256 devices in a mesh: rep: 64 (over y, z, x_lo), fsdp: 4 (over x_hi, core).
Axes of the slice: x: 4 (x_hi: 2, x_lo: 2; x = x_hi * 2 + x_lo), y: 4, z: 8, core: 2. Of those that a mesh axis runs over, the one named last changes fastest.
Arguments:
- hidden_in: bfloat16 [64, 1024, 4096], P('rep', 'fsdp'), may hold values from -36 to 36
- norm_gain: float32 [4096], replicated, may hold values from 0.1 to 1.9
- replica_weight: bfloat16 [64, 4096, 512], P('rep', 'fsdp'), may hold values from -8.8 to 8.8
- cotangent: bfloat16 [64, 1024, 512], P('rep', 'fsdp'), may hold values from -12 to 12
- adam_first: float32 [64, 4096, 512], P('rep', 'fsdp'), may hold values from -3 to 3
- adam_second: float32 [64, 4096, 512], P('rep', 'fsdp'), may hold values from 0.1 to 4
- anchor: float32 [4096, 512], P(('fsdp', 'rep')), may hold values from -4 to 4
- outer_momentum: float32 [4096, 512], P(('fsdp', 'rep')), may hold values from -1.8 to 1.8
Outputs:
- projected: bfloat16 [64, 1024, 512], P('rep', 'fsdp')
- first_moment: float32 [64, 4096, 512], P('rep', 'fsdp')
- second_moment: float32 [64, 4096, 512], P('rep', 'fsdp')
- new_anchor: float32 [4096, 512], P(('fsdp', 'rep'))
- new_momentum: float32 [4096, 512], P(('fsdp', 'rep'))
The draws below stay inside these ranges and needn't reach their ends.
All inputs are finite; a program needn't handle non-finite values.
Results may differ from the reference program's by a relative error of at most 0.0049.
Values may be sent and summed in bfloat16 or wider, within the bound.
A program may use at most 64 MiB of HBM per device.

```python
import math
from functools import partial
import jax
import jax.numpy as jnp
from jax import lax

D = 4096
KVW = 512
TOK_DEV = 256
REPLICAS = 64
TOKR = 1024


def base_field(key):
    return jnp.clip(jax.random.normal(key, (D, KVW), jnp.float32), -4.0, 4.0)


def draw_anchor(key, part):
    return base_field(key)


def draw_replica_weight(key, part):
    base = base_field(key)
    key = jax.random.fold_in(key, 11)
    key_common, key_own = jax.random.split(key)
    common = jnp.clip(0.2 * jax.random.normal(key_common, (D, KVW), jnp.float32), -0.8, 0.8)
    own = jnp.clip(jax.random.normal(key_own, (REPLICAS, D, KVW), jnp.float32), -4.0, 4.0)
    return (base[None] + common[None] + own).astype(jnp.bfloat16)


def draw_hidden_in(key, part):
    key = jax.random.fold_in(key, 7)
    key_vals, key_rows, key_cols = jax.random.split(key, 3)
    rows = jnp.exp(jax.random.uniform(key_rows, (REPLICAS, TOKR, 1), jnp.float32, jnp.log(0.3), jnp.log(3.0)))
    cols = jnp.exp(jax.random.uniform(key_cols, (D,), jnp.float32, jnp.log(0.3), jnp.log(3.0)))
    values = jnp.clip(jax.random.normal(key_vals, (REPLICAS, TOKR, D), jnp.float32), -4.0, 4.0)
    return (values * rows * cols).astype(jnp.bfloat16)


def block_levels(stream_key, shape, shards, low, high):
    loudness, own = 1.0, jax.random.fold_in(stream_key, 6)
    for dim, shards_of in shards:
        steps = jnp.exp(jax.random.uniform(jax.random.fold_in(own, dim), (shards_of,), jnp.float32, low / len(shards), high / len(shards)))
        loudness = loudness * jnp.repeat(steps, shape[dim] // shards_of).reshape([-1 if axis == dim else 1 for axis in range(len(shape))])
    return loudness


def normal_values(rng, extent, width, most, cuts=(), held_as=jnp.bfloat16):
    level = block_levels(rng, extent, cuts, -0.22, 0.18) if cuts else 1.0
    drawn = jax.random.normal(rng, extent, jnp.float32) * width * level
    return jnp.minimum(jnp.maximum(drawn, -most), most).astype(held_as)


def setup_inputs(seed: int = 0) -> dict:
    arg_keys = jax.random.split(jax.random.key(seed), 9)
    hidden_in = draw_hidden_in(jax.random.fold_in(arg_keys[8], 71), 0)
    norm_gain = jnp.clip(1.0 + 0.18 * jax.random.normal(arg_keys[1], (D,), jnp.float32), 0.1, 1.9)
    replica_weight = draw_replica_weight(jax.random.fold_in(arg_keys[8], 71), 0)
    cotangent = normal_values(arg_keys[3], (REPLICAS, TOKR, KVW), 2.0, 12.0, ((0, 64), (1, 4)))
    adam_first = normal_values(arg_keys[4], (REPLICAS, D, KVW), 0.5, 3.0, ((0, 64), (1, 4)), jnp.float32)
    adam_second = jnp.clip(jnp.exp(math.log(4.0) - 3.6888794 * jax.random.uniform(arg_keys[5], (REPLICAS, D, KVW), jnp.float32) ** block_levels(arg_keys[5], (REPLICAS, D, KVW), ((0, 64), (1, 4)), -0.2, 0.2)), 0.1, 4.0)
    anchor = draw_anchor(jax.random.fold_in(arg_keys[8], 71), 0)
    outer_momentum = normal_values(arg_keys[7], (D, KVW), 0.3, 1.8, ((0, 256),), jnp.float32)
    return {"hidden_in": hidden_in, "norm_gain": norm_gain, "replica_weight": replica_weight, "cotangent": cotangent, "adam_first": adam_first, "adam_second": adam_second, "anchor": anchor, "outer_momentum": outer_momentum}


beta_one = 0.9
beta_two = 0.95
adam_eps = 1e-08
inner_rate = 0.02
decay_rate = 0.1
nesterov_mu = 0.9
outer_rate = 0.7

def replica_pass(gain, summed, items):
    tokens, weights, grad_out, moment_in, second_in = items
    inv_root = D ** (-0.5)
    wide = tokens.astype(jnp.float32)
    square = lax.optimization_barrier(jnp.mean(wide * wide, axis=-1, keepdims=True))
    normed = (wide * lax.rsqrt(square + 1e-05) * gain).astype(jnp.bfloat16)
    projected = (jnp.dot(normed, weights, preferred_element_type=jnp.float32) * inv_root).astype(jnp.bfloat16)
    blocks_n = normed.reshape(TOKR // TOK_DEV, TOK_DEV, D).astype(jnp.float32)
    blocks_c = grad_out.reshape(TOKR // TOK_DEV, TOK_DEV, KVW).astype(jnp.float32)
    partial_sums = (jnp.einsum('btd,btk->bdk', blocks_n, blocks_c) * inv_root).astype(jnp.bfloat16)
    gradient = lax.optimization_barrier(jnp.sum(partial_sums.astype(jnp.float32), axis=0))
    moment_one = beta_one * moment_in + (1.0 - beta_one) * gradient
    moment_two = beta_two * second_in + (1.0 - beta_two) * gradient * gradient
    weights32 = weights.astype(jnp.float32)
    updated = weights32 - inner_rate * (moment_one / (jnp.sqrt(moment_two) + adam_eps) + decay_rate * weights32)
    return (summed + updated, (projected, moment_one, moment_two))

def reference(hidden_in, norm_gain, replica_weight, cotangent, adam_first, adam_second, anchor, outer_momentum):
    start_sum = jnp.zeros((D, KVW), jnp.float32)
    summed, outputs = lax.scan(partial(replica_pass, norm_gain), start_sum, (hidden_in, replica_weight, cotangent, adam_first, adam_second))
    projected, first_moment, second_moment = outputs
    mean_delta = anchor - summed / REPLICAS
    new_momentum = nesterov_mu * outer_momentum + mean_delta
    new_anchor = anchor - outer_rate * (nesterov_mu * new_momentum + mean_delta)
    return (projected, first_moment, second_moment, new_anchor, new_momentum)
```

```python
import jax
import jax.numpy as jnp
from jax import lax
from jax.experimental import pallas as pl
from jax.experimental.pallas import tpu as pltpu
from jax.sharding import PartitionSpec as P

MESH = pl.DeviceIdType.MESH
BF, F32 = jnp.bfloat16, jnp.float32

beta_one = 0.9
beta_two = 0.95
adam_eps = 1e-08
inner_rate = 0.02
decay_rate = 0.1
nesterov_mu = 0.9
outer_rate = 0.7

NY, NZ, REPLICAS = 4, 8, 64
DIST = (4, 3, 5, 2, 6, 1, 7, 0)
AHEAD = 3
LAG = 2
KV = 512


def contract_first(a, b):
    return lax.dot_general(a, b, (((0,), (0,)), ((), ())), preferred_element_type=F32)


def kernel(
    hid, gain, w, cot, a1, a2, anc, mom,
    proj_out, m1_out, m2_out, anc_out, mom_out,
    hv, gv, wv, cotall, a1v, a2v, ancv, momv, scalev, nts, nta, gsc, pacc, sib, psend, precv, pout,
    ysend, yrecv, wrecv, zsend, zrecv, xown, xrecv, ancn, momn,
    load_sem, out_sem, cot_ss, cot_rs, x_ss, x_rs, w_ss, w_rs, y_ss, y_rs, z_ss, z_rs, xl_ss, xl_rs,
    sib_ss, sib_rs, p_ss, p_rs,
):
    r, f = lax.axis_index("rep"), lax.axis_index("fsdp")
    y, z, xl = lax.div(r, 16), lax.rem(lax.div(r, 2), NZ), lax.rem(r, 2)
    xh, c = lax.div(f, 2), lax.rem(f, 2)
    inv_root = 4096 ** (-0.5)

    peers = ((1 - xh) * 2 + c, (1 - xh) * 2 + 1 - c, xh * 2 + 1 - c)
    at_fsdp = [(r, p) for p in peers]
    ypeer = [None] + [lax.rem(y + d, NY) for d in range(1, NY)]
    at_y = [None] + [((ypeer[d] * NZ + z) * 2 + xl, f) for d in range(1, NY)]
    zpeer = [lax.rem(z + d, NZ) for d in DIST]
    at_z = [((y * NZ + p) * 2 + xl, f) for p in zpeer]
    at_xl = ((y * NZ + z) * 2 + 1 - xl, f)

    def remote(src, dst, ss, rs, to):
        return pltpu.make_async_remote_copy(
            src_ref=src, dst_ref=dst, send_sem=ss, recv_sem=rs, device_id=to, device_id_type=MESH
        )

    loads = {}
    for i, (name, src, dst) in enumerate((
        ("hid", hid, hv), ("gain", gain, gv), ("w", w, wv), ("cot", cot, cotall.at[:, f]),
        ("a1", a1, a1v), ("a2", a2, a2v), ("anc", anc, ancv), ("mom", mom, momv),
    )):
        loads[name] = pltpu.make_async_copy(src, dst, load_sem.at[i])
        loads[name].start()

    barrier = pltpu.get_barrier_semaphore()
    others = at_fsdp + at_y[1:] + at_z[:-1] + [at_xl]
    for to in others:
        pl.semaphore_signal(barrier, inc=1, device_id=to, device_id_type=MESH)
    pl.semaphore_wait(barrier, len(others))

    cot_p = remote(cot, cotall.at[:, f], cot_ss.at[0], cot_rs.at[0], at_fsdp[0])
    cot_s = remote(cot, cotall.at[:, f], cot_ss.at[1], cot_rs.at[1], at_fsdp[2])
    cot_p.start()
    cot_s.start()
    w_copies = []
    for d in range(1, NY):
        cp = remote(w.at[ypeer[d]], wrecv.at[y], w_ss.at[d], w_rs.at[d], at_y[d])
        cp.start()
        w_copies.append(cp)

    loads["hid"].wait()
    loads["gain"].wait()

    def squares(j, acc):
        wide = hv[:, pl.ds(pl.multiple_of(j * 128, 128), 128)].astype(F32)
        return acc + wide * wide

    acc = lax.fori_loop(0, 32, squares, jnp.zeros((256, 128), F32))
    mean = jnp.sum(acc, axis=1, keepdims=True) * (1.0 / 4096)
    scalev[...] = jnp.broadcast_to(lax.rsqrt(mean + 1e-05), (256, 128))

    for i, owner in enumerate((*peers, f)):

        def block(j, carry, i=i, owner=owner):
            cols = pl.ds(pl.multiple_of(owner * 1024 + j * 128, 128), 128)
            wide = hv[:, cols].astype(F32)
            normed = (wide * scalev[...] * gv[:, cols]).astype(BF)
            turned = normed.T
            yy, zz = lax.div(j, 2), lax.rem(j, 2) * 4
            for h in range(2):
                part = turned[:, h * 128 : (h + 1) * 128].reshape(4, 32, 128)
                if i < 3:
                    nts[i, h, yy, pl.ds(zz, 4)] = part
                else:
                    nta[h, f, yy, pl.ds(zz, 4)] = part
            return carry

        lax.fori_loop(0, 8, block, 0)

    groups = []
    for g in range(12):
        copies = []
        for p in range(3):
            if g < 4:
                src, dst = nts.at[p, 0, g], nta.at[0, f, g]
            else:
                src, dst = nts.at[p, 1, :, zpeer[g - 4]], nta.at[1, f, :, zpeer[g - 4]]
            copies.append(remote(src, dst, x_ss.at[g, p], x_rs.at[g, p], at_fsdp[p]))
        groups.append(copies)

    def start_group(g):
        if g < len(groups):
            for cp in groups[g]:
                cp.start()

    def take_group(g):
        for cp in groups[g]:
            cp.wait_recv()
        for cp in groups[g]:
            cp.wait_send()
        start_group(g + AHEAD)

    for g in range(AHEAD):
        start_group(g)

    loads["cot"].wait()
    loads["w"].wait()
    cot_p.wait_recv()
    passed = cotall.at[:, peers[0]]
    cot_f = remote(passed, passed, cot_ss.at[2], cot_rs.at[2], at_fsdp[2])
    cot_f.start()

    def put_partial(h, part, first):
        for s in range(4):
            piece = part[:, s * 128 : (s + 1) * 128]
            if first:
                pacc[h, s] = piece
            else:
                pacc[h, s] += piece

    sib_copies, p_copies = [], []

    def to_sibling(h):
        for q, owner in enumerate((peers[2], peers[1])):
            cp = remote(pacc.at[h, owner], sib.at[h, q], sib_ss.at[h, q], sib_rs.at[h, q], at_fsdp[2])
            cp.start()
            sib_copies.append(cp)

    def to_partner(h):
        sib_copies[2 * h + 1].wait_recv()
        psend[h] = (pacc[h, peers[0]] + sib[h, 1]).astype(BF)
        cp = remote(psend.at[h], precv.at[h], p_ss.at[h], p_rs.at[h], at_fsdp[0])
        cp.start()
        p_copies.append(cp)

    for g in range(4):
        take_group(g)
        tokens = jnp.concatenate([nta[0, s, g].reshape(256, 128) for s in range(4)], axis=1)
        put_partial(0, contract_first(wv[g].reshape(256, KV), tokens), g == 0)
    to_sibling(0)

    cot_s.wait_recv()
    cot_f.wait_recv()
    loads["a1"].wait()
    loads["a2"].wait()
    to_partner(0)

    y_copies, z_copies, outs = [], [], []

    def local_out(src, dst):
        cp = pltpu.make_async_copy(src, dst, out_sem.at[len(outs)])
        cp.start()
        outs.append(cp)

    def sum_y(k):
        for cp in y_copies[k]:
            cp.wait_recv()
        steps = ysend[k, y].astype(F32)
        weights = wv[y, zpeer[k]].astype(F32)
        for d in range(1, NY):
            steps += yrecv[k, ypeer[d]].astype(F32)
            weights += wrecv[ypeer[d], zpeer[k]].astype(F32)
        total = (1.0 - inner_rate * decay_rate) * weights - inner_rate * steps
        zsend[k] = total.reshape(2, 16, KV)
        if DIST[k]:
            cp = remote(zsend.at[k], zrecv.at[k], z_ss.at[k], z_rs.at[k], at_z[k])
            cp.start()
            z_copies.append(cp)

    def chunk_tokens(k):
        parts = [
            jnp.concatenate([nta[h, s, :, zpeer[k]].reshape(128, 128) for s in range(4)], axis=1)
            for h in range(2)
        ]
        return parts

    for k in range(8):
        take_group(4 + k)
        halves = chunk_tokens(k)
        grad = jnp.dot(halves[0], cotall[0].reshape(512, KV), preferred_element_type=F32)
        grad += jnp.dot(halves[1], cotall[1].reshape(512, KV), preferred_element_type=F32)
        gsc[...] = (grad * inv_root).reshape(4, 32, KV)
        for yy in range(4):
            g = gsc[yy]
            one = beta_one * a1v[yy, zpeer[k]] + (1.0 - beta_one) * g
            two = beta_two * a2v[yy, zpeer[k]] + (1.0 - beta_two) * g * g
            a1v[yy, zpeer[k]] = one
            a2v[yy, zpeer[k]] = two
            ysend[k, yy] = (one / (jnp.sqrt(two) + adam_eps)).astype(BF)
        copies = []
        for d in range(1, NY):
            cp = remote(ysend.at[k, ypeer[d]], yrecv.at[k, y], y_ss.at[k, d], y_rs.at[k, d], at_y[d])
            cp.start()
            copies.append(cp)
        y_copies.append(copies)
        local_out(a1v.at[:, zpeer[k]], m1_out.at[:, zpeer[k]])
        local_out(a2v.at[:, zpeer[k]], m2_out.at[:, zpeer[k]])
        if k % 2:
            tokens = jnp.concatenate([chunk_tokens(k - 1)[1], halves[1]], axis=0)
            weights = jnp.concatenate(
                [wv[:, zpeer[k - 1]].reshape(128, KV), wv[:, zpeer[k]].reshape(128, KV)], axis=0
            )
            put_partial(1, contract_first(weights, tokens), k == 1)
        if k == 7:
            to_sibling(1)
        if k == LAG:
            for cp in w_copies:
                cp.wait_recv()
        if k >= LAG:
            sum_y(k - LAG)

    to_partner(1)
    for k in range(8 - LAG, 8):
        sum_y(k)

    total = zsend[7]
    for cp, k in zip(z_copies, range(7)):
        cp.wait_recv()
        total += zrecv[k]
    xown[...] = total
    cp_xl = remote(xown.at[1 - xl], xrecv, xl_ss, xl_rs, at_xl)
    cp_xl.start()

    def finish(h):
        sib_copies[2 * h].wait_recv()
        p_copies[h].wait_recv()
        whole = (pacc[h, f] + sib[h, 0] + precv[h].astype(F32)) * inv_root
        pout[h] = whole.astype(BF).T
        local_out(pout.at[h], proj_out.at[h])

    finish(0)
    cp_xl.wait_recv()
    loads["anc"].wait()
    loads["mom"].wait()
    mean_delta = ancv[...] - (xown[xl] + xrecv[...]) * (1.0 / REPLICAS)
    new_momentum = nesterov_mu * momv[...] + mean_delta
    momn[...] = new_momentum
    ancn[...] = ancv[...] - outer_rate * (nesterov_mu * new_momentum + mean_delta)
    local_out(momn, mom_out)
    local_out(ancn, anc_out)
    finish(1)

    for cp in [cot_p, cot_s, cot_f, *w_copies, *sum(y_copies, []), *z_copies, *sib_copies, *p_copies, cp_xl]:
        cp.wait_send()
    for cp in outs:
        cp.wait()


def per_device(
    hidden_in, norm_gain, replica_weight, cotangent, adam_first, adam_second, anchor, outer_momentum
):
    any_space = pl.BlockSpec(memory_space=pl.ANY)
    dma = pltpu.SemaphoreType.DMA
    rows = (NY, NZ, 32)
    outs = pl.pallas_call(
        kernel,
        name="diloco_step",
        out_shape=(
            jax.ShapeDtypeStruct((2, 128, KV), BF),
            jax.ShapeDtypeStruct((*rows, KV), F32),
            jax.ShapeDtypeStruct((*rows, KV), F32),
            jax.ShapeDtypeStruct((16, KV), F32),
            jax.ShapeDtypeStruct((16, KV), F32),
        ),
        in_specs=[any_space] * 8,
        out_specs=[any_space] * 5,
        scratch_shapes=[
            pltpu.VMEM((256, 4096), BF),
            pltpu.VMEM((1, 4096), F32),
            pltpu.VMEM((*rows, KV), BF),
            pltpu.VMEM((2, 4, 128, KV), BF),
            pltpu.VMEM((*rows, KV), F32),
            pltpu.VMEM((*rows, KV), F32),
            pltpu.VMEM((16, KV), F32),
            pltpu.VMEM((16, KV), F32),
            pltpu.VMEM((256, 128), F32),
            pltpu.VMEM((3, 2, *rows, 128), BF),
            pltpu.VMEM((2, 4, *rows, 128), BF),
            pltpu.VMEM((4, 32, KV), F32),
            pltpu.VMEM((2, 4, KV, 128), F32),
            pltpu.VMEM((2, 2, KV, 128), F32),
            pltpu.VMEM((2, KV, 128), BF),
            pltpu.VMEM((2, KV, 128), BF),
            pltpu.VMEM((2, 128, KV), BF),
            pltpu.VMEM((8, NY, 32, KV), BF),
            pltpu.VMEM((8, NY, 32, KV), BF),
            pltpu.VMEM((NY, NZ, 32, KV), BF),
            pltpu.VMEM((8, 2, 16, KV), F32),
            pltpu.VMEM((8, 2, 16, KV), F32),
            pltpu.VMEM((2, 16, KV), F32),
            pltpu.VMEM((16, KV), F32),
            pltpu.VMEM((16, KV), F32),
            pltpu.VMEM((16, KV), F32),
            dma((8,)),
            dma((20,)),
            dma((3,)), dma((3,)),
            dma((12, 3)), dma((12, 3)),
            dma((NY,)), dma((NY,)),
            dma((8, NY)), dma((8, NY)),
            dma((8,)), dma((8,)),
            dma, dma,
            dma((2, 2)), dma((2, 2)),
            dma((2,)), dma((2,)),
        ],
        compiler_params=pltpu.CompilerParams(
            collective_id=0, has_side_effects=True, vmem_limit_bytes=56 << 20
        ),
        cost_estimate=pl.CostEstimate(
            flops=4 * 256 * 4096 * 512, bytes_accessed=12 << 20, transcendentals=1 << 20
        ),
    )(
        hidden_in.reshape(256, 4096),
        norm_gain.reshape(1, 4096),
        replica_weight.reshape(*rows, KV),
        cotangent.reshape(2, 128, KV),
        adam_first.reshape(*rows, KV),
        adam_second.reshape(*rows, KV),
        anchor,
        outer_momentum,
    )
    projected, first, second, new_anchor, new_momentum = outs
    return (
        projected.reshape(1, 256, KV),
        first.reshape(1, 1024, KV),
        second.reshape(1, 1024, KV),
        new_anchor,
        new_momentum,
    )


def solution(mesh):
    placed = (
        P("rep", "fsdp", None),
        P(),
        P("rep", "fsdp", None),
        P("rep", "fsdp", None),
        P("rep", "fsdp", None),
        P("rep", "fsdp", None),
        P(("fsdp", "rep"), None),
        P(("fsdp", "rep"), None),
    )
    return jax.shard_map(
        per_device,
        mesh=mesh,
        in_specs=placed,
        out_specs=(
            P("rep", "fsdp", None),
            P("rep", "fsdp", None),
            P("rep", "fsdp", None),
            P(("fsdp", "rep"), None),
            P(("fsdp", "rep"), None),
        ),
        check_vma=False,
    )
```

```python
import jax
import jax.numpy as jnp
from jax import lax
from jax.experimental import pallas as pl
from jax.experimental.pallas import tpu as pltpu
from jax.sharding import PartitionSpec as P

MESH = pl.DeviceIdType.MESH
BF, F32 = jnp.bfloat16, jnp.float32

beta_one = 0.9
beta_two = 0.95
adam_eps = 1e-08
inner_rate = 0.02
decay_rate = 0.1
nesterov_mu = 0.9
outer_rate = 0.7

NY, NZ, REPLICAS = 4, 8, 64
DIST = (4, 3, 5, 2, 6, 1, 7, 0)
AHEAD = 3
LAG = 2
KV = 512
PIECES = 2
PK = KV // PIECES


def contract_first(a, b):
    return lax.dot_general(a, b, (((0,), (0,)), ((), ())), preferred_element_type=F32)


def kernel(
    hid, gain, w, cot, a1, a2, anc, mom,
    pout, m1v, m2v, ancn, momn,
    hv, gv, wv, cotall, a1v, a2v, ancv, momv, scalev, nts, nta, gsc, pacc, sib, psend, precv,
    ysend, yrecv, wrecv, zsend, zrecv, xown, xrecv,
    load_sem, cot_ss, cot_rs, x_ss, x_rs, w_ss, w_rs, y_ss, y_rs, z_ss, z_rs, xl_ss, xl_rs,
    sib_ss, sib_rs, p_ss, p_rs,
):
    r, f = lax.axis_index("rep"), lax.axis_index("fsdp")
    y, z, xl = lax.div(r, 16), lax.rem(lax.div(r, 2), NZ), lax.rem(r, 2)
    xh, c = lax.div(f, 2), lax.rem(f, 2)
    inv_root = 4096 ** (-0.5)

    peers = ((1 - xh) * 2 + c, (1 - xh) * 2 + 1 - c, xh * 2 + 1 - c)
    at_fsdp = [(r, p) for p in peers]
    ypeer = [None] + [lax.rem(y + d, NY) for d in range(1, NY)]
    at_y = [None] + [((ypeer[d] * NZ + z) * 2 + xl, f) for d in range(1, NY)]
    at_z = [((y * NZ + lax.rem(z + d, NZ)) * 2 + xl, f) for d in DIST]

    def owner_z(k):
        return lax.rem(z + 4 + lax.div(k + 1, 2) * (1 - 2 * lax.rem(k, 2)), NZ)

    at_xl = ((y * NZ + z) * 2 + 1 - xl, f)

    def remote(src, dst, ss, rs, to):
        return pltpu.make_async_remote_copy(
            src_ref=src, dst_ref=dst, send_sem=ss, recv_sem=rs, device_id=to, device_id_type=MESH
        )

    barrier = pltpu.get_barrier_semaphore()
    others = at_fsdp + at_y[1:] + at_z[:-1] + [at_xl]
    for to in others:
        pl.semaphore_signal(barrier, inc=1, device_id=to, device_id_type=MESH)

    loads = {}
    for i, (name, src, dst) in enumerate((
        ("hid", hid, hv), ("gain", gain, gv), ("w", w, wv), ("cot", cot, cotall.at[:, f]),
        ("a1", a1, a1v), ("a2", a2, a2v), ("anc", anc, ancv), ("mom", mom, momv),
    )):
        loads[name] = pltpu.make_async_copy(src, dst, load_sem.at[i])
        loads[name].start()

    pl.semaphore_wait(barrier, len(others))

    cot_p = remote(cot, cotall.at[:, f], cot_ss.at[0], cot_rs.at[0], at_fsdp[0])
    cot_s = remote(cot, cotall.at[:, f], cot_ss.at[1], cot_rs.at[1], at_fsdp[2])
    cot_p.start()
    cot_s.start()
    w_copies = []
    for d in range(1, NY):
        cp = remote(w.at[ypeer[d]], wrecv.at[y], w_ss.at[d], w_rs.at[d], at_y[d])
        cp.start()
        w_copies.append(cp)

    loads["hid"].wait()
    loads["gain"].wait()

    def squares(j, acc):
        wide = hv[:, pl.ds(pl.multiple_of(j * 128, 128), 128)].astype(F32)
        return acc + wide * wide

    acc = lax.fori_loop(0, 32, squares, jnp.zeros((256, 128), F32))
    mean = jnp.sum(acc, axis=1, keepdims=True) * (1.0 / 4096)
    scalev[...] = jnp.broadcast_to(lax.rsqrt(mean + 1e-05), (256, 128))

    def turn(owner, j):
        cols = pl.ds(pl.multiple_of(owner * 1024 + j * 128, 128), 128)
        wide = hv[:, cols].astype(F32)
        turned = (wide * scalev[...] * gv[:, cols]).astype(BF).T
        return [turned[:, h * 128 : (h + 1) * 128].reshape(4, 32, 128) for h in range(2)]

    def block_for_peer(n, carry):
        i, j = lax.div(n, 8), lax.rem(n, 8)
        up, side = lax.div(i, 2), lax.div(i + 1, 2)
        owner = ((1 - xh) * (1 - up) + xh * up) * 2 + c * (1 - side) + (1 - c) * side
        for h, part in enumerate(turn(owner, j)):
            nts[i, h, lax.div(j, 2), pl.ds(lax.rem(j, 2) * 4, 4)] = part
        return carry

    def block_for_me(j, carry):
        for h, part in enumerate(turn(f, j)):
            nta[h, f, lax.div(j, 2), pl.ds(lax.rem(j, 2) * 4, 4)] = part
        return carry

    lax.fori_loop(0, 24, block_for_peer, 0)

    def x_copy(k, h, p):
        zz = owner_z(k)
        return remote(nts.at[p, h, :, zz], nta.at[h, f, :, zz], x_ss.at[k, h, p], x_rs.at[k, h, p], at_fsdp[p])

    def start_group(g):
        late = lax.div(g, 6)
        for n in range(2):
            k, h = g * (1 - late) + (6 + n) * late, n * (1 - late) + (g - 6) * late
            for p in range(3):
                x_copy(k, h, p).start()

    def take(k, h):
        for p in range(3):
            x_copy(k, h, p).wait_recv()

    def start_first(g, carry):
        start_group(g)
        return carry

    lax.fori_loop(0, AHEAD, start_first, 0)
    lax.fori_loop(0, 8, block_for_me, 0)
    pacc[...] = jnp.zeros_like(pacc)

    loads["cot"].wait()
    loads["w"].wait()
    cot_p.wait_recv()
    passed = cotall.at[:, peers[0]]
    cot_f = remote(passed, passed, cot_ss.at[2], cot_rs.at[2], at_fsdp[2])
    cot_f.start()

    def sib_copy(h, q, i):
        rows = pl.ds(i * PK, PK)
        owner = (peers[2], peers[1])[q]
        return remote(
            pacc.at[h, owner, rows], sib.at[h, q, rows], sib_ss.at[h, q, i], sib_rs.at[h, q, i], at_fsdp[2]
        )

    def p_copy(h, i):
        rows = pl.ds(i * PK, PK)
        return remote(psend.at[h, rows], precv.at[h, rows], p_ss.at[h, i], p_rs.at[h, i], at_fsdp[0])

    def to_partner(h):
        def piece(i, carry):
            rows = pl.ds(i * PK, PK)
            sib_copy(h, 1, i).wait_recv()
            psend[h, rows] = (pacc[h, peers[0], rows] + sib[h, 1, rows]).astype(BF)
            p_copy(h, i).start()
            return carry

        lax.fori_loop(0, PIECES, piece, 0)

    def chunk_tokens(k, h):
        zz = owner_z(k)
        return jnp.concatenate([nta[h, s, :, zz].reshape(128, 128) for s in range(4)], axis=1)

    def pair_partial(k, h, rows, n):
        tokens = jnp.concatenate([chunk_tokens(k - 1, h), chunk_tokens(k, h)], axis=0)
        weights = jnp.concatenate([wv[:, owner_z(j), :, rows].reshape(128, n) for j in (k - 1, k)], axis=0)
        part = contract_first(weights, tokens)
        for s in range(4):
            pacc[h, s, rows] += part[:, s * 128 : (s + 1) * 128]

    def last_partial(h):
        def piece(i, carry):
            pair_partial(7, h, pl.ds(pl.multiple_of(i * PK, PK), PK), PK)
            sib_copy(h, 1, i).start()
            sib_copy(h, 0, i).start()
            return carry

        lax.fori_loop(0, PIECES, piece, 0)

    cot_s.wait_recv()
    cot_f.wait_recv()
    loads["a1"].wait()
    loads["a2"].wait()

    def y_copy(k, d):
        return remote(ysend.at[k, ypeer[d]], yrecv.at[k, y], y_ss.at[k, d], y_rs.at[k, d], at_y[d])

    def z_copy(k):
        to = ((y * NZ + owner_z(k)) * 2 + xl, f)
        return remote(zsend.at[k], zrecv.at[k], z_ss.at[k], z_rs.at[k], to)

    def sum_y(k, own=False):
        for d in range(1, NY):
            y_copy(k, d).wait_recv()
        zz = owner_z(k)
        steps = ysend[k, y].astype(F32)
        weights = wv[y, zz].astype(F32)
        for d in range(1, NY):
            steps += yrecv[k, ypeer[d]].astype(F32)
            weights += wrecv[ypeer[d], zz].astype(F32)
        total = (1.0 - inner_rate * decay_rate) * weights - inner_rate * steps
        zsend[k] = total.reshape(2, 16, KV)
        if not own:
            z_copy(k).start()

    def inner_step(k):
        zz = owner_z(k)
        grad = jnp.dot(chunk_tokens(k, 0), cotall[0].reshape(512, KV), preferred_element_type=F32)
        grad += jnp.dot(chunk_tokens(k, 1), cotall[1].reshape(512, KV), preferred_element_type=F32)
        gsc[...] = (grad * inv_root).reshape(4, 32, KV)

        def rows(yy, carry):
            g = gsc[yy]
            one = beta_one * a1v[yy, zz] + (1.0 - beta_one) * g
            two = beta_two * a2v[yy, zz] + (1.0 - beta_two) * g * g
            m1v[yy, zz] = one
            m2v[yy, zz] = two
            ysend[k, yy] = (one / (jnp.sqrt(two) + adam_eps)).astype(BF)
            return carry

        lax.fori_loop(0, 4, rows, 0)
        for d in range(1, NY):
            y_copy(k, d).start()

    def early(k, carry):
        take(k, 0)
        take(k, 1)

        @pl.when(k + AHEAD < 8)
        def _():
            start_group(k + AHEAD)

        inner_step(k)

        @pl.when(k == LAG)
        def _():
            for cp in w_copies:
                cp.wait_recv()

        @pl.when(k >= LAG)
        def _():
            sum_y(k - LAG)

        @pl.when(lax.rem(k, 2) == 1)
        def _():
            def half(h, inner):
                pair_partial(k, h, slice(None), KV)
                return inner

            lax.fori_loop(0, 2, half, 0)

        return carry

    lax.fori_loop(0, 6, early, 0)
    take(6, 0)
    take(7, 0)
    last_partial(0)

    def late(k, carry):
        take(k, 1)

        @pl.when(k == 7)
        def _():
            to_partner(0)

        inner_step(k)
        sum_y(k - LAG)
        return carry

    lax.fori_loop(6, 8, late, 0)
    last_partial(1)
    sum_y(6)
    to_partner(1)
    sum_y(7, own=True)

    def add_z(k, total):
        z_copy(k).wait_recv()
        return total + zrecv[k]

    total = lax.fori_loop(0, 7, add_z, zsend[7])
    xown[...] = total
    cp_xl = remote(xown.at[1 - xl], xrecv, xl_ss, xl_rs, at_xl)
    cp_xl.start()

    def finish(h):
        def piece(i, carry):
            rows = pl.ds(pl.multiple_of(i * PK, PK), PK)
            sib_copy(h, 0, i).wait_recv()
            p_copy(h, i).wait_recv()
            whole = (pacc[h, f, rows] + sib[h, 0, rows] + precv[h, rows].astype(F32)) * inv_root
            pout[h, :, rows] = whole.astype(BF).T
            return carry

        lax.fori_loop(0, PIECES, piece, 0)

    finish(0)
    cp_xl.wait_recv()
    loads["anc"].wait()
    loads["mom"].wait()
    mean_delta = ancv[...] - (xown[xl] + xrecv[...]) * (1.0 / REPLICAS)
    new_momentum = nesterov_mu * momv[...] + mean_delta
    momn[...] = new_momentum
    ancn[...] = ancv[...] - outer_rate * (nesterov_mu * new_momentum + mean_delta)
    finish(1)

    for cp in [cot_p, cot_s, cot_f, *w_copies, cp_xl]:
        cp.wait_send()

    def sent(k, carry):
        for h in range(2):
            for p in range(3):
                x_copy(k, h, p).wait_send()
        for d in range(1, NY):
            y_copy(k, d).wait_send()

        @pl.when(k < 7)
        def _():
            z_copy(k).wait_send()

        return carry

    lax.fori_loop(0, 8, sent, 0)
    for h in range(2):
        for i in range(PIECES):
            for q in range(2):
                sib_copy(h, q, i).wait_send()
            p_copy(h, i).wait_send()


def write_out(*refs):
    copies = [pltpu.make_async_copy(refs[i], refs[5 + i], refs[10].at[i]) for i in range(5)]
    for cp in copies:
        cp.start()
    for cp in copies:
        cp.wait()


def per_device(
    hidden_in, norm_gain, replica_weight, cotangent, adam_first, adam_second, anchor, outer_momentum
):
    any_space = pl.BlockSpec(memory_space=pl.ANY)
    dma = pltpu.SemaphoreType.DMA
    in_vmem = pl.BlockSpec(memory_space=pltpu.VMEM)
    rows = (NY, NZ, 32)
    results = [((2, 128, KV), BF), ((*rows, KV), F32), ((*rows, KV), F32), ((16, KV), F32), ((16, KV), F32)]
    outs = pl.pallas_call(
        kernel,
        name="diloco_step",
        out_shape=tuple(pltpu.VMEM(*o) for o in results),
        in_specs=[any_space] * 8,
        out_specs=[in_vmem] * 5,
        scratch_shapes=[
            pltpu.VMEM((256, 4096), BF),
            pltpu.VMEM((1, 4096), F32),
            pltpu.VMEM((*rows, KV), BF),
            pltpu.VMEM((2, 4, 128, KV), BF),
            pltpu.VMEM((*rows, KV), F32),
            pltpu.VMEM((*rows, KV), F32),
            pltpu.VMEM((16, KV), F32),
            pltpu.VMEM((16, KV), F32),
            pltpu.VMEM((256, 128), F32),
            pltpu.VMEM((3, 2, *rows, 128), BF),
            pltpu.VMEM((2, 4, *rows, 128), BF),
            pltpu.VMEM((4, 32, KV), F32),
            pltpu.VMEM((2, 4, KV, 128), F32),
            pltpu.VMEM((2, 2, KV, 128), F32),
            pltpu.VMEM((2, KV, 128), BF),
            pltpu.VMEM((2, KV, 128), BF),
            pltpu.VMEM((8, NY, 32, KV), BF),
            pltpu.VMEM((8, NY, 32, KV), BF),
            pltpu.VMEM((NY, NZ, 32, KV), BF),
            pltpu.VMEM((8, 2, 16, KV), F32),
            pltpu.VMEM((8, 2, 16, KV), F32),
            pltpu.VMEM((2, 16, KV), F32),
            pltpu.VMEM((16, KV), F32),
            dma((8,)),
            dma((3,)), dma((3,)),
            dma((8, 2, 3)), dma((8, 2, 3)),
            dma((NY,)), dma((NY,)),
            dma((8, NY)), dma((8, NY)),
            dma((8,)), dma((8,)),
            dma, dma,
            dma((2, 2, PIECES)), dma((2, 2, PIECES)),
            dma((2, PIECES)), dma((2, PIECES)),
        ],
        compiler_params=pltpu.CompilerParams(
            collective_id=0, has_side_effects=True, vmem_limit_bytes=52 << 20
        ),
        cost_estimate=pl.CostEstimate(
            flops=4 * 256 * 4096 * 512, bytes_accessed=12 << 20, transcendentals=1 << 20
        ),
    )(
        hidden_in.reshape(256, 4096),
        norm_gain.reshape(1, 4096),
        replica_weight.reshape(*rows, KV),
        cotangent.reshape(2, 128, KV),
        adam_first.reshape(*rows, KV),
        adam_second.reshape(*rows, KV),
        anchor,
        outer_momentum,
    )
    projected, first, second, new_anchor, new_momentum = pl.pallas_call(
        write_out,
        name="write_out",
        out_shape=tuple(jax.ShapeDtypeStruct(*o) for o in results),
        in_specs=[in_vmem] * 5,
        out_specs=[any_space] * 5,
        scratch_shapes=[dma((5,))],
        compiler_params=pltpu.CompilerParams(vmem_limit_bytes=1 << 20),
        cost_estimate=pl.CostEstimate(flops=0, bytes_accessed=5 << 20, transcendentals=0),
    )(*(pltpu.with_memory_space_constraint(o, pltpu.VMEM) for o in outs))
    return (
        projected.reshape(1, 256, KV),
        first.reshape(1, 1024, KV),
        second.reshape(1, 1024, KV),
        new_anchor,
        new_momentum,
    )


def solution(mesh):
    placed = (
        P("rep", "fsdp", None),
        P(),
        P("rep", "fsdp", None),
        P("rep", "fsdp", None),
        P("rep", "fsdp", None),
        P("rep", "fsdp", None),
        P(("fsdp", "rep"), None),
        P(("fsdp", "rep"), None),
    )
    return jax.shard_map(
        per_device,
        mesh=mesh,
        in_specs=placed,
        out_specs=(
            P("rep", "fsdp", None),
            P("rep", "fsdp", None),
            P("rep", "fsdp", None),
            P(("fsdp", "rep"), None),
            P(("fsdp", "rep"), None),
        ),
        check_vma=False,
    )
```

```python
import jax
import jax.numpy as jnp
from jax import lax
from jax.experimental import pallas as pl
from jax.experimental.pallas import tpu as pltpu
from jax.sharding import PartitionSpec as P

MESH = pl.DeviceIdType.MESH
BF, F32 = jnp.bfloat16, jnp.float32

beta_one = 0.9
beta_two = 0.95
adam_eps = 1e-08
inner_rate = 0.02
decay_rate = 0.1
nesterov_mu = 0.9
outer_rate = 0.7

NY, NZ, REPLICAS = 4, 8, 64
DIST = (4, 3, 5, 2, 6, 1, 7, 0)
AHEAD = 3
LAG = 2
KV = 512
PIECES = 2
PK = KV // PIECES


def contract_first(a, b):
    return lax.dot_general(a, b, (((0,), (0,)), ((), ())), preferred_element_type=F32)


def kernel(
    hid, gain, w, cot, a1, a2, anc, mom,
    pout, m1v, m2v, ancn, momn,
    hv, gv, wv, cotall, a1v, a2v, ancv, momv, scalev, nts, nta, gsc, pacc, sib, psend, precv,
    ysend, yrecv, ylast, wrecv, zsend, zrecv, xown, xrecv,
    load_sem, cot_ss, cot_rs, x_ss, x_rs, w_ss, w_rs, y_ss, y_rs, yl_ss, yl_rs, z_ss, z_rs, xl_ss, xl_rs,
    sib_ss, sib_rs, p_ss, p_rs,
):
    r, f = lax.axis_index("rep"), lax.axis_index("fsdp")
    y, z, xl = lax.div(r, 16), lax.rem(lax.div(r, 2), NZ), lax.rem(r, 2)
    xh, c = lax.div(f, 2), lax.rem(f, 2)
    inv_root = 4096 ** (-0.5)

    peers = ((1 - xh) * 2 + c, (1 - xh) * 2 + 1 - c, xh * 2 + 1 - c)
    at_fsdp = [(r, p) for p in peers]
    ypeer = [None] + [lax.rem(y + d, NY) for d in range(1, NY)]
    at_y = [None] + [((ypeer[d] * NZ + z) * 2 + xl, f) for d in range(1, NY)]
    at_z = [((y * NZ + lax.rem(z + d, NZ)) * 2 + xl, f) for d in DIST]

    def owner_z(k):
        return lax.rem(z + 4 + lax.div(k + 1, 2) * (1 - 2 * lax.rem(k, 2)), NZ)

    both_xl = (xl, 1 - xl)
    last_to = [(d, e) for d in range(NY) for e in range(2) if d + e]
    yring = [y] + ypeer[1:]

    def at_last(d, e):
        return ((yring[d] * NZ + z) * 2 + both_xl[e], f)

    at_xl = at_last(0, 1)

    def remote(src, dst, ss, rs, to):
        return pltpu.make_async_remote_copy(
            src_ref=src, dst_ref=dst, send_sem=ss, recv_sem=rs, device_id=to, device_id_type=MESH
        )

    barrier = pltpu.get_barrier_semaphore()
    others = at_fsdp + at_z[:-1] + [at_last(*t) for t in last_to]
    for to in others:
        pl.semaphore_signal(barrier, inc=1, device_id=to, device_id_type=MESH)

    def arrived(region, sem):
        pltpu.make_async_copy(region, region, sem).wait()

    loads = {}
    for i, (name, src, dst) in enumerate((
        ("hid", hid, hv), ("gain", gain, gv), ("w", w, wv), ("cot", cot, cotall.at[:, f]),
        ("a1", a1, a1v), ("a2", a2, a2v), ("anc", anc, ancv), ("mom", mom, momv),
    )):
        loads[name] = pltpu.make_async_copy(src, dst, load_sem.at[i])
        if name not in ("a1", "a2", "anc", "mom"):
            loads[name].start()

    pl.semaphore_wait(barrier, len(others))

    cot_p = remote(cot, cotall.at[:, f], cot_ss.at[0], cot_rs.at[0], at_fsdp[0])
    cot_s = remote(cot, cotall.at[:, f], cot_ss.at[1], cot_rs.at[1], at_fsdp[2])
    cot_p.start()
    cot_s.start()
    for d in range(1, NY):
        cp = remote(w.at[ypeer[d]], wrecv.at[y], w_ss, w_rs, at_y[d])
        cp.start()

    loads["hid"].wait()
    loads["gain"].wait()
    for name in ("a1", "a2", "anc", "mom"):
        loads[name].start()

    def squares(j, acc):
        wide = hv[:, pl.ds(pl.multiple_of(j * 128, 128), 128)].astype(F32)
        return acc + wide * wide

    acc = lax.fori_loop(0, 32, squares, jnp.zeros((256, 128), F32))
    mean = jnp.sum(acc, axis=1, keepdims=True) * (1.0 / 4096)
    scalev[...] = jnp.broadcast_to(lax.rsqrt(mean + 1e-05), (256, 128))

    def turn(owner, j):
        cols = pl.ds(pl.multiple_of(owner * 1024 + j * 128, 128), 128)
        wide = hv[:, cols].astype(F32)
        turned = (wide * scalev[...] * gv[:, cols]).astype(BF).T
        return [turned[:, h * 128 : (h + 1) * 128].reshape(4, 32, 128) for h in range(2)]

    def block_for_peer(n, carry):
        i, j = lax.div(n, 8), lax.rem(n, 8)
        up, side = lax.div(i, 2), lax.div(i + 1, 2)
        owner = ((1 - xh) * (1 - up) + xh * up) * 2 + c * (1 - side) + (1 - c) * side
        for h, part in enumerate(turn(owner, j)):
            nts[i, h, lax.div(j, 2), pl.ds(lax.rem(j, 2) * 4, 4)] = part
        return carry

    def block_for_me(j, carry):
        for h, part in enumerate(turn(f, j)):
            nta[h, f, lax.div(j, 2), pl.ds(lax.rem(j, 2) * 4, 4)] = part
        return carry

    lax.fori_loop(0, 24, block_for_peer, 0)

    def start(k):
        zz = owner_z(k)
        for p in range(3):
            remote(nts.at[p, :, :, zz], nta.at[:, f, :, zz], x_ss, x_rs.at[k], at_fsdp[p]).start()

    def start_half(h):
        for p in range(3):
            remote(nts.at[p, h, :, z], nta.at[h, f, :, z], x_ss, x_rs.at[7 + h], at_fsdp[p]).start()

    def take(k):
        arrived(nts.at[:, :, :, 0], x_rs.at[k])

    def take_half(h):
        arrived(nts.at[:, h, :, 0], x_rs.at[7 + h])

    def start_first(k, carry):
        start(k)
        return carry

    lax.fori_loop(0, AHEAD, start_first, 0)
    lax.fori_loop(0, 8, block_for_me, 0)
    pacc[...] = jnp.zeros_like(pacc)

    loads["cot"].wait()
    loads["w"].wait()
    cot_p.wait_recv()
    passed = cotall.at[:, peers[0]]
    cot_f = remote(passed, passed, cot_ss.at[2], cot_rs.at[2], at_fsdp[2])
    cot_f.start()

    def sib_copy(h, q, i):
        rows = pl.ds(i * PK, PK)
        owner = (peers[2], peers[1])[q]
        return remote(
            pacc.at[h, owner, rows], sib.at[h, q, rows], sib_ss, sib_rs.at[h, q, i], at_fsdp[2]
        )

    def p_copy(h, i):
        rows = pl.ds(i * PK, PK)
        return remote(psend.at[h, rows], precv.at[h, rows], p_ss, p_rs.at[h, i], at_fsdp[0])

    def to_partner(h):
        def piece(i, carry):
            rows = pl.ds(i * PK, PK)
            sib_copy(h, 1, i).wait_recv()
            psend[h, rows] = (pacc[h, peers[0], rows] + sib[h, 1, rows]).astype(BF)
            p_copy(h, i).start()
            return carry

        lax.fori_loop(0, PIECES, piece, 0)

    def chunk_tokens(k, h):
        zz = owner_z(k)
        return jnp.concatenate([nta[h, s, :, zz].reshape(128, 128) for s in range(4)], axis=1)

    def pair_partial(k, h, rows, n):
        tokens = jnp.concatenate([chunk_tokens(k - 1, h), chunk_tokens(k, h)], axis=0)
        weights = jnp.concatenate([wv[:, owner_z(j), :, rows].reshape(128, n) for j in (k - 1, k)], axis=0)
        part = contract_first(weights, tokens)
        for s in range(4):
            pacc[h, s, rows] += part[:, s * 128 : (s + 1) * 128]

    def last_partial(h):
        def piece(i, carry):
            pair_partial(7, h, pl.ds(pl.multiple_of(i * PK, PK), PK), PK)
            sib_copy(h, 1, i).start()
            sib_copy(h, 0, i).start()
            return carry

        lax.fori_loop(0, PIECES, piece, 0)

    cot_s.wait_recv()
    cot_f.wait_recv()
    loads["a1"].wait()
    loads["a2"].wait()

    def y_copy(k, d):
        return remote(ysend.at[k, ypeer[d]], yrecv.at[k, y], y_ss, y_rs.at[k], at_y[d])

    def z_copy(k):
        to = ((y * NZ + owner_z(k)) * 2 + xl, f)
        return remote(zsend.at[k], zrecv.at[k], z_ss, z_rs, to)

    def yl_copy(d, e):
        src = ysend.at[7, yring[d], both_xl[e]]
        return remote(src, ylast.at[y, xl], yl_ss, yl_rs, at_last(d, e))

    def sum_weights(zz):
        weights = wv[y, zz].astype(F32)
        for d in range(1, NY):
            weights += wrecv[ypeer[d], zz].astype(F32)
        return (1.0 - inner_rate * decay_rate) * weights.reshape(2, 16, KV)

    def sum_y(k):
        arrived(yrecv.at[k, 0:3], y_rs.at[k])
        steps = ysend[k, y].astype(F32)
        for d in range(1, NY):
            steps += yrecv[k, ypeer[d]].astype(F32)
        zsend[k] = sum_weights(owner_z(k)) - inner_rate * steps
        z_copy(k).start()

    def inner_step(k, last=False):
        zz = owner_z(k)
        grad = jnp.dot(chunk_tokens(k, 0), cotall[0].reshape(512, KV), preferred_element_type=F32)
        grad += jnp.dot(chunk_tokens(k, 1), cotall[1].reshape(512, KV), preferred_element_type=F32)
        gsc[...] = (grad * inv_root).reshape(4, 32, KV)

        def rows(yy, carry):
            g = gsc[yy]
            one = beta_one * a1v[yy, zz] + (1.0 - beta_one) * g
            two = beta_two * a2v[yy, zz] + (1.0 - beta_two) * g * g
            m1v[yy, zz] = one
            m2v[yy, zz] = two
            ysend[k, yy] = (one / (jnp.sqrt(two) + adam_eps)).astype(BF).reshape(2, 16, KV)
            return carry

        lax.fori_loop(0, 4, rows, 0)
        for copy in [yl_copy(*t) for t in last_to] if last else [y_copy(k, d) for d in range(1, NY)]:
            copy.start()

    def early(k, carry):
        take(k)

        @pl.when(k + AHEAD < 7)
        def _():
            start(k + AHEAD)

        for h in range(2):

            @pl.when(k + AHEAD == 7 + h)
            def _(h=h):
                start_half(h)

        inner_step(k)

        @pl.when(k == LAG)
        def _():
            arrived(wv.at[0:3], w_rs)

        @pl.when(k >= LAG)
        def _():
            sum_y(k - LAG)

        @pl.when(lax.rem(k, 2) == 1)
        def _():
            def half(h, inner):
                pair_partial(k, h, slice(None), KV)
                return inner

            lax.fori_loop(0, 2, half, 0)

        return carry

    lax.fori_loop(0, 7, early, 0)
    take_half(0)
    last_partial(0)
    sum_y(5)
    take_half(1)
    to_partner(0)
    inner_step(7, last=True)
    last_partial(1)
    sum_y(6)
    to_partner(1)

    def add_z(k, total):
        return total + zrecv[k]

    arrived(zrecv, z_rs)

    total = lax.fori_loop(0, 7, add_z, sum_weights(z))
    xown[...] = total
    cp_xl = remote(xown.at[1 - xl], xrecv, xl_ss, xl_rs, at_xl)
    cp_xl.start()

    def finish(h):
        def piece(i, carry):
            rows = pl.ds(pl.multiple_of(i * PK, PK), PK)
            sib_copy(h, 0, i).wait_recv()
            p_copy(h, i).wait_recv()
            whole = (pacc[h, f, rows] + sib[h, 0, rows] + precv[h, rows].astype(F32)) * inv_root
            pout[h, :, rows] = whole.astype(BF).T
            return carry

        lax.fori_loop(0, PIECES, piece, 0)

    finish(0)
    cp_xl.wait_recv()
    loads["anc"].wait()
    loads["mom"].wait()
    steps = ysend[7, y, xl].astype(F32)
    arrived(ysend.at[0:7, 0, 0], yl_rs)
    for d, e in last_to:
        steps += ylast[yring[d], both_xl[e]].astype(F32)
    mean_delta = ancv[...] - (xown[xl] + xrecv[...] - inner_rate * steps) * (1.0 / REPLICAS)
    new_momentum = nesterov_mu * momv[...] + mean_delta
    momn[...] = new_momentum
    ancn[...] = ancv[...] - outer_rate * (nesterov_mu * new_momentum + mean_delta)
    finish(1)

    for cp in [cot_p, cot_s, cot_f, cp_xl]:
        cp.wait_send()
    arrived(wv.at[0:3], w_ss)
    arrived(nts, x_ss)
    arrived(yrecv.at[:, 0:3], y_ss)
    arrived(ysend.at[0:7, 0, 0], yl_ss)
    arrived(zsend, z_ss)
    arrived(sib, sib_ss)
    arrived(psend, p_ss)


def write_out(*refs):
    copies = [pltpu.make_async_copy(refs[i], refs[5 + i], refs[10].at[i]) for i in range(5)]
    for cp in copies:
        cp.start()
    for cp in copies:
        cp.wait()


def per_device(
    hidden_in, norm_gain, replica_weight, cotangent, adam_first, adam_second, anchor, outer_momentum
):
    any_space = pl.BlockSpec(memory_space=pl.ANY)
    dma = pltpu.SemaphoreType.DMA
    in_vmem = pl.BlockSpec(memory_space=pltpu.VMEM)
    rows = (NY, NZ, 32)
    results = [((2, 128, KV), BF), ((*rows, KV), F32), ((*rows, KV), F32), ((16, KV), F32), ((16, KV), F32)]
    outs = pl.pallas_call(
        kernel,
        name="diloco_step",
        out_shape=tuple(pltpu.VMEM(*o) for o in results),
        in_specs=[any_space] * 8,
        out_specs=[in_vmem] * 5,
        scratch_shapes=[
            pltpu.VMEM((256, 4096), BF),
            pltpu.VMEM((1, 4096), F32),
            pltpu.VMEM((*rows, KV), BF),
            pltpu.VMEM((2, 4, 128, KV), BF),
            pltpu.VMEM((*rows, KV), F32),
            pltpu.VMEM((*rows, KV), F32),
            pltpu.VMEM((16, KV), F32),
            pltpu.VMEM((16, KV), F32),
            pltpu.VMEM((256, 128), F32),
            pltpu.VMEM((3, 2, *rows, 128), BF),
            pltpu.VMEM((2, 4, *rows, 128), BF),
            pltpu.VMEM((4, 32, KV), F32),
            pltpu.VMEM((2, 4, KV, 128), F32),
            pltpu.VMEM((2, 2, KV, 128), F32),
            pltpu.VMEM((2, KV, 128), BF),
            pltpu.VMEM((2, KV, 128), BF),
            pltpu.VMEM((8, NY, 2, 16, KV), BF),
            pltpu.VMEM((7, NY, 2, 16, KV), BF),
            pltpu.VMEM((NY, 2, 16, KV), BF),
            pltpu.VMEM((NY, NZ, 32, KV), BF),
            pltpu.VMEM((7, 2, 16, KV), F32),
            pltpu.VMEM((7, 2, 16, KV), F32),
            pltpu.VMEM((2, 16, KV), F32),
            pltpu.VMEM((16, KV), F32),
            dma((8,)),
            dma((3,)), dma((3,)),
            dma, dma((9,)),
            dma, dma,
            dma, dma((7,)),
            dma, dma,
            dma, dma,
            dma, dma,
            dma, dma((2, 2, PIECES)),
            dma, dma((2, PIECES)),
        ],
        compiler_params=pltpu.CompilerParams(
            collective_id=0, has_side_effects=True, vmem_limit_bytes=52 << 20
        ),
        cost_estimate=pl.CostEstimate(
            flops=4 * 256 * 4096 * 512, bytes_accessed=12 << 20, transcendentals=1 << 20
        ),
    )(
        hidden_in.reshape(256, 4096),
        norm_gain.reshape(1, 4096),
        replica_weight.reshape(*rows, KV),
        cotangent.reshape(2, 128, KV),
        adam_first.reshape(*rows, KV),
        adam_second.reshape(*rows, KV),
        anchor,
        outer_momentum,
    )
    projected, first, second, new_anchor, new_momentum = pl.pallas_call(
        write_out,
        name="write_out",
        out_shape=tuple(jax.ShapeDtypeStruct(*o) for o in results),
        in_specs=[in_vmem] * 5,
        out_specs=[any_space] * 5,
        scratch_shapes=[dma((5,))],
        compiler_params=pltpu.CompilerParams(vmem_limit_bytes=1 << 20),
        cost_estimate=pl.CostEstimate(flops=0, bytes_accessed=5 << 20, transcendentals=0),
    )(*(pltpu.with_memory_space_constraint(o, pltpu.VMEM) for o in outs))
    return (
        projected.reshape(1, 256, KV),
        first.reshape(1, 1024, KV),
        second.reshape(1, 1024, KV),
        new_anchor,
        new_momentum,
    )


def solution(mesh):
    placed = (
        P("rep", "fsdp", None),
        P(),
        P("rep", "fsdp", None),
        P("rep", "fsdp", None),
        P("rep", "fsdp", None),
        P("rep", "fsdp", None),
        P(("fsdp", "rep"), None),
        P(("fsdp", "rep"), None),
    )
    return jax.shard_map(
        per_device,
        mesh=mesh,
        in_specs=placed,
        out_specs=(
            P("rep", "fsdp", None),
            P("rep", "fsdp", None),
            P("rep", "fsdp", None),
            P(("fsdp", "rep"), None),
            P(("fsdp", "rep"), None),
        ),
        check_vma=False,
    )
```

```python
import jax
import jax.numpy as jnp
from jax import lax
from jax.experimental import pallas as pl
from jax.experimental.pallas import tpu as pltpu
from jax.sharding import PartitionSpec as P

MESH = pl.DeviceIdType.MESH
BF, F32 = jnp.bfloat16, jnp.float32

beta_one = 0.9
beta_two = 0.95
adam_eps = 1e-08
inner_rate = 0.02
decay_rate = 0.1
nesterov_mu = 0.9
outer_rate = 0.7

NY, NZ, REPLICAS = 4, 8, 64
DIST = (4, 3, 5, 2, 6, 1, 7, 0)
AHEAD = 3
LAG = 2
KV = 512
PIECES = 1
PK = KV // PIECES


def contract_first(a, b):
    return lax.dot_general(a, b, (((0,), (0,)), ((), ())), preferred_element_type=F32)


def kernel(
    hid, gain, w, cot, a1, a2, anc, mom,
    pout, m1v, m2v, ancn, momn,
    hv, gv, wv, cotall, a1v, a2v, ancv, momv, scalev, nts, nta, gsc, pacc, sib, psend, precv,
    ysend, yrecv, ylast, wrecv, zsend, zrecv, xown, xrecv,
    load_sem, cot_ss, cot_rs, x_ss, x_rs, w_ss, w_rs, y_ss, y_rs, yl_ss, yl_rs, z_ss, z_rs, xl_ss, xl_rs,
    sib_ss, sib_rs, p_ss, p_rs,
):
    r, f = lax.axis_index("rep"), lax.axis_index("fsdp")
    y, z, xl = lax.div(r, 16), lax.rem(lax.div(r, 2), NZ), lax.rem(r, 2)
    xh, c = lax.div(f, 2), lax.rem(f, 2)
    inv_root = 4096 ** (-0.5)

    peers = ((1 - xh) * 2 + c, (1 - xh) * 2 + 1 - c, xh * 2 + 1 - c)
    at_fsdp = [(r, p) for p in peers]
    ypeer = [None] + [lax.rem(y + d, NY) for d in range(1, NY)]
    at_y = [None] + [((ypeer[d] * NZ + z) * 2 + xl, f) for d in range(1, NY)]
    at_z = [((y * NZ + lax.rem(z + d, NZ)) * 2 + xl, f) for d in DIST]

    def owner_z(k):
        return lax.rem(z + 4 + lax.div(k + 1, 2) * (1 - 2 * lax.rem(k, 2)), NZ)

    both_xl = (xl, 1 - xl)
    last_to = [(d, e) for d in range(NY) for e in range(2) if d + e]
    yring = [y] + ypeer[1:]

    def at_last(d, e):
        return ((yring[d] * NZ + z) * 2 + both_xl[e], f)

    at_xl = at_last(0, 1)

    def remote(src, dst, ss, rs, to):
        return pltpu.make_async_remote_copy(
            src_ref=src, dst_ref=dst, send_sem=ss, recv_sem=rs, device_id=to, device_id_type=MESH
        )

    barrier = pltpu.get_barrier_semaphore()
    others = at_fsdp + at_z[:-1] + [at_last(*t) for t in last_to]
    for to in others:
        pl.semaphore_signal(barrier, inc=1, device_id=to, device_id_type=MESH)

    def arrived(region, sem):
        pltpu.make_async_copy(region, region, sem).wait()

    loads = {}
    for i, (name, src, dst) in enumerate((
        ("hid", hid, hv), ("gain", gain, gv), ("w", w, wv), ("cot", cot, cotall.at[:, f]),
        ("a1", a1, a1v), ("a2", a2, a2v), ("anc", anc, ancv), ("mom", mom, momv),
    )):
        loads[name] = pltpu.make_async_copy(src, dst, load_sem.at[i])
        if name not in ("a1", "a2", "anc", "mom"):
            loads[name].start()

    pl.semaphore_wait(barrier, len(others))

    cot_p = remote(cot, cotall.at[:, f], cot_ss.at[0], cot_rs.at[0], at_fsdp[0])
    cot_s = remote(cot, cotall.at[:, f], cot_ss.at[1], cot_rs.at[1], at_fsdp[2])
    cot_p.start()
    cot_s.start()
    for d in range(1, NY):
        cp = remote(w.at[ypeer[d]], wrecv.at[y], w_ss, w_rs, at_y[d])
        cp.start()

    loads["hid"].wait()
    loads["gain"].wait()
    for name in ("a1", "a2", "anc", "mom"):
        loads[name].start()

    def squares(j, acc):
        wide = hv[:, pl.ds(pl.multiple_of(j * 128, 128), 128)].astype(F32)
        return acc + wide * wide

    acc = lax.fori_loop(0, 32, squares, jnp.zeros((256, 128), F32))
    mean = jnp.sum(acc, axis=1, keepdims=True) * (1.0 / 4096)
    scalev[...] = jnp.broadcast_to(lax.rsqrt(mean + 1e-05), (256, 128))

    def turn(owner, j):
        cols = pl.ds(pl.multiple_of(owner * 1024 + j * 128, 128), 128)
        wide = hv[:, cols].astype(F32)
        turned = (wide * scalev[...] * gv[:, cols]).astype(BF).T
        return [turned[:, h * 128 : (h + 1) * 128].reshape(4, 32, 128) for h in range(2)]

    def block_for_peer(n, carry):
        i, j = lax.div(n, 8), lax.rem(n, 8)
        up, side = lax.div(i, 2), lax.div(i + 1, 2)
        owner = ((1 - xh) * (1 - up) + xh * up) * 2 + c * (1 - side) + (1 - c) * side
        for h, part in enumerate(turn(owner, j)):
            nts[i, h, lax.div(j, 2), pl.ds(lax.rem(j, 2) * 4, 4)] = part
        return carry

    def block_for_me(j, carry):
        for h, part in enumerate(turn(f, j)):
            nta[h, f, lax.div(j, 2), pl.ds(lax.rem(j, 2) * 4, 4)] = part
        return carry

    lax.fori_loop(0, 24, block_for_peer, 0)

    def start(k):
        zz = owner_z(k)
        for p in range(3):
            remote(nts.at[p, :, :, zz], nta.at[:, f, :, zz], x_ss, x_rs.at[k], at_fsdp[p]).start()

    def start_half(h):
        for p in range(3):
            remote(nts.at[p, h, :, z], nta.at[h, f, :, z], x_ss, x_rs.at[7 + h], at_fsdp[p]).start()

    def take(k):
        arrived(nts.at[:, :, :, 0], x_rs.at[k])

    def take_half(h):
        arrived(nts.at[:, h, :, 0], x_rs.at[7 + h])

    def start_first(k, carry):
        start(k)
        return carry

    lax.fori_loop(0, AHEAD, start_first, 0)
    lax.fori_loop(0, 8, block_for_me, 0)
    pacc[...] = jnp.zeros_like(pacc)

    loads["cot"].wait()
    loads["w"].wait()
    cot_p.wait_recv()
    passed = cotall.at[:, peers[0]]
    cot_f = remote(passed, passed, cot_ss.at[2], cot_rs.at[2], at_fsdp[2])
    cot_f.start()

    def sib_copy(h, q, i):
        rows = pl.ds(i * PK, PK)
        owner = (peers[2], peers[1])[q]
        return remote(
            pacc.at[h, owner, rows], sib.at[h, q, rows], sib_ss, sib_rs.at[h, q, i], at_fsdp[2]
        )

    def p_copy(h, i):
        rows = pl.ds(i * PK, PK)
        return remote(psend.at[h, rows], precv.at[h, rows], p_ss, p_rs.at[h, i], at_fsdp[0])

    def to_partner(h):
        def piece(i, carry):
            rows = pl.ds(i * PK, PK)
            sib_copy(h, 1, i).wait_recv()
            psend[h, rows] = (pacc[h, peers[0], rows] + sib[h, 1, rows]).astype(BF)
            p_copy(h, i).start()
            return carry

        lax.fori_loop(0, PIECES, piece, 0)

    def chunk_tokens(k, h):
        zz = owner_z(k)
        return jnp.concatenate([nta[h, s, :, zz].reshape(128, 128) for s in range(4)], axis=1)

    def pair_partial(k, h, rows, n):
        tokens = jnp.concatenate([chunk_tokens(k - 1, h), chunk_tokens(k, h)], axis=0)
        weights = jnp.concatenate([wv[:, owner_z(j), :, rows].reshape(128, n) for j in (k - 1, k)], axis=0)
        part = contract_first(weights, tokens)
        for s in range(4):
            pacc[h, s, rows] += part[:, s * 128 : (s + 1) * 128]

    def last_partial(h):
        def piece(i, carry):
            pair_partial(7, h, pl.ds(pl.multiple_of(i * PK, PK), PK), PK)
            sib_copy(h, 1, i).start()
            sib_copy(h, 0, i).start()
            return carry

        lax.fori_loop(0, PIECES, piece, 0)

    cot_s.wait_recv()
    cot_f.wait_recv()
    loads["a1"].wait()
    loads["a2"].wait()

    def y_copy(k, d):
        return remote(ysend.at[k, ypeer[d]], yrecv.at[k, y], y_ss, y_rs.at[k], at_y[d])

    def z_copy(k):
        to = ((y * NZ + owner_z(k)) * 2 + xl, f)
        return remote(zsend.at[k], zrecv.at[k], z_ss, z_rs, to)

    def yl_copy(d, e):
        src = ysend.at[7, yring[d], both_xl[e]]
        return remote(src, ylast.at[y, xl], yl_ss, yl_rs, at_last(d, e))

    def sum_weights(zz):
        weights = wv[y, zz].astype(F32)
        for d in range(1, NY):
            weights += wrecv[ypeer[d], zz].astype(F32)
        return (1.0 - inner_rate * decay_rate) * weights.reshape(2, 16, KV)

    def sum_y(k):
        arrived(yrecv.at[k, 0:3], y_rs.at[k])
        steps = ysend[k, y].astype(F32)
        for d in range(1, NY):
            steps += yrecv[k, ypeer[d]].astype(F32)
        zsend[k] = sum_weights(owner_z(k)) - inner_rate * steps
        z_copy(k).start()

    def inner_step(k, last=False):
        zz = owner_z(k)
        grad = jnp.dot(chunk_tokens(k, 0), cotall[0].reshape(512, KV), preferred_element_type=F32)
        grad += jnp.dot(chunk_tokens(k, 1), cotall[1].reshape(512, KV), preferred_element_type=F32)
        gsc[...] = (grad * inv_root).reshape(4, 32, KV)

        def rows(yy, carry):
            g = gsc[yy]
            one = beta_one * a1v[yy, zz] + (1.0 - beta_one) * g
            two = beta_two * a2v[yy, zz] + (1.0 - beta_two) * g * g
            m1v[yy, zz] = one
            m2v[yy, zz] = two
            ysend[k, yy] = (one / (jnp.sqrt(two) + adam_eps)).astype(BF).reshape(2, 16, KV)
            return carry

        lax.fori_loop(0, 4, rows, 0)
        for copy in [yl_copy(*t) for t in last_to] if last else [y_copy(k, d) for d in range(1, NY)]:
            copy.start()

    def early(k, carry):
        take(k)

        @pl.when(k + AHEAD < 7)
        def _():
            start(k + AHEAD)

        for h in range(2):

            @pl.when(k + AHEAD == 7 + h)
            def _(h=h):
                start_half(h)

        inner_step(k)

        @pl.when(k == LAG)
        def _():
            arrived(wv.at[0:3], w_rs)

        @pl.when(k >= LAG)
        def _():
            sum_y(k - LAG)

        @pl.when(lax.rem(k, 2) == 1)
        def _():
            def half(h, inner):
                pair_partial(k, h, slice(None), KV)
                return inner

            lax.fori_loop(0, 2, half, 0)

        return carry

    lax.fori_loop(0, 7, early, 0)
    take_half(0)
    last_partial(0)
    sum_y(5)
    to_partner(0)
    take_half(1)
    inner_step(7, last=True)
    last_partial(1)
    sum_y(6)
    to_partner(1)

    def add_z(k, total):
        return total + zrecv[k]

    arrived(zrecv, z_rs)

    total = lax.fori_loop(0, 7, add_z, sum_weights(z))
    xown[...] = total
    cp_xl = remote(xown.at[1 - xl], xrecv, xl_ss, xl_rs, at_xl)
    cp_xl.start()

    def finish(h):
        def piece(i, carry):
            rows = pl.ds(pl.multiple_of(i * PK, PK), PK)
            sib_copy(h, 0, i).wait_recv()
            p_copy(h, i).wait_recv()
            whole = (pacc[h, f, rows] + sib[h, 0, rows] + precv[h, rows].astype(F32)) * inv_root
            pout[h, :, rows] = whole.astype(BF).T
            return carry

        lax.fori_loop(0, PIECES, piece, 0)

    finish(0)
    cp_xl.wait_recv()
    loads["anc"].wait()
    loads["mom"].wait()
    steps = ysend[7, y, xl].astype(F32)
    arrived(ysend.at[0:7, 0, 0], yl_rs)
    for d, e in last_to:
        steps += ylast[yring[d], both_xl[e]].astype(F32)
    mean_delta = ancv[...] - (xown[xl] + xrecv[...] - inner_rate * steps) * (1.0 / REPLICAS)
    new_momentum = nesterov_mu * momv[...] + mean_delta
    momn[...] = new_momentum
    ancn[...] = ancv[...] - outer_rate * (nesterov_mu * new_momentum + mean_delta)
    finish(1)

    for cp in [cot_p, cot_s, cot_f, cp_xl]:
        cp.wait_send()
    arrived(wv.at[0:3], w_ss)
    arrived(nts, x_ss)
    arrived(yrecv.at[:, 0:3], y_ss)
    arrived(ysend.at[0:7, 0, 0], yl_ss)
    arrived(zsend, z_ss)
    arrived(sib, sib_ss)
    arrived(psend, p_ss)


def write_out(*refs):
    copies = [pltpu.make_async_copy(refs[i], refs[5 + i], refs[10].at[i]) for i in range(5)]
    for cp in copies:
        cp.start()
    for cp in copies:
        cp.wait()


def per_device(
    hidden_in, norm_gain, replica_weight, cotangent, adam_first, adam_second, anchor, outer_momentum
):
    any_space = pl.BlockSpec(memory_space=pl.ANY)
    dma = pltpu.SemaphoreType.DMA
    in_vmem = pl.BlockSpec(memory_space=pltpu.VMEM)
    rows = (NY, NZ, 32)
    results = [((2, 128, KV), BF), ((*rows, KV), F32), ((*rows, KV), F32), ((16, KV), F32), ((16, KV), F32)]
    outs = pl.pallas_call(
        kernel,
        name="diloco_step",
        out_shape=tuple(pltpu.VMEM(*o) for o in results),
        in_specs=[any_space] * 8,
        out_specs=[in_vmem] * 5,
        scratch_shapes=[
            pltpu.VMEM((256, 4096), BF),
            pltpu.VMEM((1, 4096), F32),
            pltpu.VMEM((*rows, KV), BF),
            pltpu.VMEM((2, 4, 128, KV), BF),
            pltpu.VMEM((*rows, KV), F32),
            pltpu.VMEM((*rows, KV), F32),
            pltpu.VMEM((16, KV), F32),
            pltpu.VMEM((16, KV), F32),
            pltpu.VMEM((256, 128), F32),
            pltpu.VMEM((3, 2, *rows, 128), BF),
            pltpu.VMEM((2, 4, *rows, 128), BF),
            pltpu.VMEM((4, 32, KV), F32),
            pltpu.VMEM((2, 4, KV, 128), F32),
            pltpu.VMEM((2, 2, KV, 128), F32),
            pltpu.VMEM((2, KV, 128), BF),
            pltpu.VMEM((2, KV, 128), BF),
            pltpu.VMEM((8, NY, 2, 16, KV), BF),
            pltpu.VMEM((7, NY, 2, 16, KV), BF),
            pltpu.VMEM((NY, 2, 16, KV), BF),
            pltpu.VMEM((NY, NZ, 32, KV), BF),
            pltpu.VMEM((7, 2, 16, KV), F32),
            pltpu.VMEM((7, 2, 16, KV), F32),
            pltpu.VMEM((2, 16, KV), F32),
            pltpu.VMEM((16, KV), F32),
            dma((8,)),
            dma((3,)), dma((3,)),
            dma, dma((9,)),
            dma, dma,
            dma, dma((7,)),
            dma, dma,
            dma, dma,
            dma, dma,
            dma, dma((2, 2, PIECES)),
            dma, dma((2, PIECES)),
        ],
        compiler_params=pltpu.CompilerParams(
            collective_id=0, has_side_effects=True, vmem_limit_bytes=52 << 20
        ),
        cost_estimate=pl.CostEstimate(
            flops=4 * 256 * 4096 * 512, bytes_accessed=12 << 20, transcendentals=1 << 20
        ),
    )(
        hidden_in.reshape(256, 4096),
        norm_gain.reshape(1, 4096),
        replica_weight.reshape(*rows, KV),
        cotangent.reshape(2, 128, KV),
        adam_first.reshape(*rows, KV),
        adam_second.reshape(*rows, KV),
        anchor,
        outer_momentum,
    )
    projected, first, second, new_anchor, new_momentum = pl.pallas_call(
        write_out,
        name="write_out",
        out_shape=tuple(jax.ShapeDtypeStruct(*o) for o in results),
        in_specs=[in_vmem] * 5,
        out_specs=[any_space] * 5,
        scratch_shapes=[dma((5,))],
        compiler_params=pltpu.CompilerParams(vmem_limit_bytes=1 << 20),
        cost_estimate=pl.CostEstimate(flops=0, bytes_accessed=5 << 20, transcendentals=0),
    )(*(pltpu.with_memory_space_constraint(o, pltpu.VMEM) for o in outs))
    return (
        projected.reshape(1, 256, KV),
        first.reshape(1, 1024, KV),
        second.reshape(1, 1024, KV),
        new_anchor,
        new_momentum,
    )


def solution(mesh):
    placed = (
        P("rep", "fsdp", None),
        P(),
        P("rep", "fsdp", None),
        P("rep", "fsdp", None),
        P("rep", "fsdp", None),
        P("rep", "fsdp", None),
        P(("fsdp", "rep"), None),
        P(("fsdp", "rep"), None),
    )
    return jax.shard_map(
        per_device,
        mesh=mesh,
        in_specs=placed,
        out_specs=(
            P("rep", "fsdp", None),
            P("rep", "fsdp", None),
            P("rep", "fsdp", None),
            P(("fsdp", "rep"), None),
            P(("fsdp", "rep"), None),
        ),
        check_vma=False,
    )
```

```python
import jax
import jax.numpy as jnp
from jax import lax
from jax.experimental import pallas as pl
from jax.experimental.pallas import tpu as pltpu
from jax.sharding import PartitionSpec as P

MESH = pl.DeviceIdType.MESH
BF, F32 = jnp.bfloat16, jnp.float32

beta_one = 0.9
beta_two = 0.95
adam_eps = 1e-08
inner_rate = 0.02
decay_rate = 0.1
nesterov_mu = 0.9
outer_rate = 0.7

NY, NZ, REPLICAS = 4, 8, 64
DIST = (4, 3, 5, 2, 6, 1, 7, 0)
AHEAD = 3
LAG = 2
KV = 512
PIECES = 1
PK = KV // PIECES


def contract_first(a, b):
    return lax.dot_general(a, b, (((0,), (0,)), ((), ())), preferred_element_type=F32)


def kernel(
    hid, gain, w, cot, a1, a2, anc, mom,
    pout, m1v, m2v, ancn, momn,
    hv, gv, wv, cotall, a1v, a2v, ancv, momv, scalev, nts, nta, gsc, pacc, sib, psend, precv,
    ysend, yrecv, ylast, wrecv, zsend, zrecv, xown, xrecv,
    load_sem, cot_ss, cot_rs, x_ss, x_rs, w_ss, w_rs, y_ss, y_rs, yl_ss, yl_rs, z_ss, z_rs, xl_ss, xl_rs,
    sib_ss, sib_rs, p_ss, p_rs,
):
    r, f = lax.axis_index("rep"), lax.axis_index("fsdp")
    y, z, xl = lax.div(r, 16), lax.rem(lax.div(r, 2), NZ), lax.rem(r, 2)
    xh, c = lax.div(f, 2), lax.rem(f, 2)
    inv_root = 4096 ** (-0.5)

    peers = ((1 - xh) * 2 + c, (1 - xh) * 2 + 1 - c, xh * 2 + 1 - c)
    at_fsdp = [(r, p) for p in peers]
    ypeer = [None] + [lax.rem(y + d, NY) for d in range(1, NY)]
    at_y = [None] + [((ypeer[d] * NZ + z) * 2 + xl, f) for d in range(1, NY)]
    at_z = [((y * NZ + lax.rem(z + d, NZ)) * 2 + xl, f) for d in DIST]

    def owner_z(k):
        return lax.rem(z + 4 + lax.div(k + 1, 2) * (1 - 2 * lax.rem(k, 2)), NZ)

    both_xl = (xl, 1 - xl)
    last_to = [(d, e) for d in range(NY) for e in range(2) if d + e]
    yring = [y] + ypeer[1:]

    def at_last(d, e):
        return ((yring[d] * NZ + z) * 2 + both_xl[e], f)

    at_xl = at_last(0, 1)

    def remote(src, dst, ss, rs, to):
        return pltpu.make_async_remote_copy(
            src_ref=src, dst_ref=dst, send_sem=ss, recv_sem=rs, device_id=to, device_id_type=MESH
        )

    barrier = pltpu.get_barrier_semaphore()
    others = at_fsdp + at_z[:-1] + [at_last(*t) for t in last_to]
    for to in others:
        pl.semaphore_signal(barrier, inc=1, device_id=to, device_id_type=MESH)

    def arrived(region, sem):
        pltpu.make_async_copy(region, region, sem).wait()

    loads = {}
    for i, (name, src, dst) in enumerate((
        ("hid", hid, hv), ("gain", gain, gv), ("w", w, wv), ("cot", cot, cotall.at[:, f]),
        ("a1", a1, a1v), ("a2", a2, a2v), ("anc", anc, ancv), ("mom", mom, momv),
    )):
        loads[name] = pltpu.make_async_copy(src, dst, load_sem.at[i])
        if name not in ("a1", "a2", "anc", "mom"):
            loads[name].start()

    pl.semaphore_wait(barrier, len(others))

    cot_p = remote(cot, cotall.at[:, f], cot_ss.at[0], cot_rs.at[0], at_fsdp[0])
    cot_s = remote(cot, cotall.at[:, f], cot_ss.at[1], cot_rs.at[1], at_fsdp[2])
    cot_p.start()
    cot_s.start()
    for d in range(1, NY):
        cp = remote(w.at[ypeer[d]], wrecv.at[y], w_ss, w_rs, at_y[d])
        cp.start()

    loads["hid"].wait()
    loads["gain"].wait()
    for name in ("a1", "a2", "anc", "mom"):
        loads[name].start()

    def squares(j, acc):
        wide = hv[:, pl.ds(pl.multiple_of(j * 128, 128), 128)].astype(F32)
        return acc + wide * wide

    acc = lax.fori_loop(0, 32, squares, jnp.zeros((256, 128), F32))
    mean = jnp.sum(acc, axis=1, keepdims=True) * (1.0 / 4096)
    scalev[...] = jnp.broadcast_to(lax.rsqrt(mean + 1e-05), (256, 128))

    def turn(owner, j):
        cols = pl.ds(pl.multiple_of(owner * 1024 + j * 128, 128), 128)
        wide = hv[:, cols].astype(F32)
        turned = (wide * scalev[...] * gv[:, cols]).astype(BF).T
        return [turned[:, h * 128 : (h + 1) * 128].reshape(4, 32, 128) for h in range(2)]

    def block_for_peer(n, carry):
        i, j = lax.div(n, 8), lax.rem(n, 8)
        up, side = lax.div(i, 2), lax.div(i + 1, 2)
        owner = ((1 - xh) * (1 - up) + xh * up) * 2 + c * (1 - side) + (1 - c) * side
        for h, part in enumerate(turn(owner, j)):
            nts[i, h, lax.div(j, 2), pl.ds(lax.rem(j, 2) * 4, 4)] = part
        return carry

    def block_for_me(j, carry):
        for h, part in enumerate(turn(f, j)):
            nta[h, f, lax.div(j, 2), pl.ds(lax.rem(j, 2) * 4, 4)] = part
        return carry

    lax.fori_loop(0, 24, block_for_peer, 0)

    def start(k):
        zz = owner_z(k)
        for p in range(3):
            remote(nts.at[p, :, :, zz], nta.at[:, f, :, zz], x_ss, x_rs.at[k], at_fsdp[p]).start()

    def start_half(h):
        for p in range(3):
            remote(nts.at[p, h, :, z], nta.at[h, f, :, z], x_ss, x_rs.at[7 + h], at_fsdp[p]).start()

    def take(k):
        arrived(nts.at[:, :, :, 0], x_rs.at[k])

    def take_half(h):
        arrived(nts.at[:, h, :, 0], x_rs.at[7 + h])

    def start_first(k, carry):
        start(k)
        return carry

    lax.fori_loop(0, AHEAD, start_first, 0)
    lax.fori_loop(0, 8, block_for_me, 0)
    pacc[...] = jnp.zeros_like(pacc)

    loads["cot"].wait()
    loads["w"].wait()
    cot_p.wait_recv()
    passed = cotall.at[:, peers[0]]
    cot_f = remote(passed, passed, cot_ss.at[2], cot_rs.at[2], at_fsdp[2])
    cot_f.start()

    def sib_copy(h, q, i):
        rows = pl.ds(i * PK, PK)
        owner = (peers[2], peers[1])[q]
        return remote(
            pacc.at[h, owner, rows], sib.at[h, q, rows], sib_ss, sib_rs.at[h, q, i], at_fsdp[2]
        )

    def p_copy(h, i):
        rows = pl.ds(i * PK, PK)
        return remote(psend.at[h, rows], precv.at[h, rows], p_ss, p_rs.at[h, i], at_fsdp[0])

    def to_partner(h):
        def piece(i, carry):
            rows = pl.ds(i * PK, PK)
            sib_copy(h, 1, i).wait_recv()
            psend[h, rows] = (pacc[h, peers[0], rows] + sib[h, 1, rows]).astype(BF)
            p_copy(h, i).start()
            return carry

        lax.fori_loop(0, PIECES, piece, 0)

    def chunk_tokens(k, h):
        zz = owner_z(k)
        return jnp.concatenate([nta[h, s, :, zz].reshape(128, 128) for s in range(4)], axis=1)

    def pair_partial(k, h, rows, n):
        tokens = jnp.concatenate([chunk_tokens(k - 1, h), chunk_tokens(k, h)], axis=0)
        weights = jnp.concatenate([wv[:, owner_z(j), :, rows].reshape(128, n) for j in (k - 1, k)], axis=0)
        part = contract_first(weights, tokens)
        for s in range(4):
            pacc[h, s, rows] += part[:, s * 128 : (s + 1) * 128]

    def last_partial(h):
        def piece(i, carry):
            pair_partial(7, h, pl.ds(pl.multiple_of(i * PK, PK), PK), PK)
            sib_copy(h, 1, i).start()
            sib_copy(h, 0, i).start()
            return carry

        lax.fori_loop(0, PIECES, piece, 0)

    cot_s.wait_recv()
    cot_f.wait_recv()
    loads["a1"].wait()
    loads["a2"].wait()

    def y_copy(k, d):
        return remote(ysend.at[k, ypeer[d]], yrecv.at[k, y], y_ss, y_rs.at[k], at_y[d])

    def z_copy(k):
        to = ((y * NZ + owner_z(k)) * 2 + xl, f)
        return remote(zsend.at[k], zrecv.at[k], z_ss, z_rs, to)

    def yl_copy(d, e):
        src = ysend.at[7, yring[d], both_xl[e]]
        return remote(src, ylast.at[y, xl], yl_ss, yl_rs, at_last(d, e))

    def sum_weights(zz):
        weights = wv[y, zz].astype(F32)
        for d in range(1, NY):
            weights += wrecv[ypeer[d], zz].astype(F32)
        return (1.0 - inner_rate * decay_rate) * weights.reshape(2, 16, KV)

    def sum_y(k):
        arrived(yrecv.at[k, 0:3], y_rs.at[k])
        steps = ysend[k, y].astype(F32)
        for d in range(1, NY):
            steps += yrecv[k, ypeer[d]].astype(F32)
        zsend[k] = sum_weights(owner_z(k)) - inner_rate * steps
        z_copy(k).start()

    def inner_step(k, last=False):
        zz = owner_z(k)
        grad = jnp.dot(chunk_tokens(k, 0), cotall[0].reshape(512, KV), preferred_element_type=F32)
        grad += jnp.dot(chunk_tokens(k, 1), cotall[1].reshape(512, KV), preferred_element_type=F32)
        gsc[...] = (grad * inv_root).reshape(4, 32, KV)

        def rows(yy, carry):
            g = gsc[yy]
            one = beta_one * a1v[yy, zz] + (1.0 - beta_one) * g
            two = beta_two * a2v[yy, zz] + (1.0 - beta_two) * g * g
            m1v[yy, zz] = one
            m2v[yy, zz] = two
            ysend[k, yy] = (one / (jnp.sqrt(two) + adam_eps)).astype(BF).reshape(2, 16, KV)
            return carry

        lax.fori_loop(0, 4, rows, 0)
        for copy in [yl_copy(*t) for t in last_to] if last else [y_copy(k, d) for d in range(1, NY)]:
            copy.start()

    def early(k, carry):
        take(k)

        @pl.when(k + AHEAD < 7)
        def _():
            start(k + AHEAD)

        for h in range(2):

            @pl.when(k + AHEAD == 7 + h)
            def _(h=h):
                start_half(h)

        inner_step(k)

        @pl.when(k == LAG)
        def _():
            arrived(wv.at[0:3], w_rs)

        @pl.when(k >= LAG)
        def _():
            sum_y(k - LAG)

        @pl.when(lax.rem(k, 2) == 1)
        def _():
            def half(h, inner):
                pair_partial(k, h, slice(None), KV)
                return inner

            lax.fori_loop(0, 2, half, 0)

        return carry

    lax.fori_loop(0, 7, early, 0)
    take_half(0)
    last_partial(0)
    sum_y(5)
    to_partner(0)
    take_half(1)
    inner_step(7, last=True)
    last_partial(1)
    sum_y(6)
    to_partner(1)

    def add_z(k, total):
        return total + zrecv[k]

    base = sum_weights(z)
    for cp in [cot_p, cot_s, cot_f]:
        cp.wait_send()
    arrived(wv.at[0:3], w_ss)
    arrived(nts, x_ss)
    arrived(yrecv.at[:, 0:3], y_ss)
    loads["anc"].wait()
    loads["mom"].wait()
    arrived(zrecv, z_rs)

    total = lax.fori_loop(0, 7, add_z, base)
    xown[...] = total
    cp_xl = remote(xown.at[1 - xl], xrecv, xl_ss, xl_rs, at_xl)
    cp_xl.start()

    def finish(h):
        def piece(i, carry):
            rows = pl.ds(pl.multiple_of(i * PK, PK), PK)
            sib_copy(h, 0, i).wait_recv()
            p_copy(h, i).wait_recv()
            whole = (pacc[h, f, rows] + sib[h, 0, rows] + precv[h, rows].astype(F32)) * inv_root
            pout[h, :, rows] = whole.astype(BF).T
            return carry

        lax.fori_loop(0, PIECES, piece, 0)

    finish(0)
    cp_xl.wait_recv()
    steps = ysend[7, y, xl].astype(F32)
    arrived(ysend.at[0:7, 0, 0], yl_rs)
    for d, e in last_to:
        steps += ylast[yring[d], both_xl[e]].astype(F32)
    mean_delta = ancv[...] - (xown[xl] + xrecv[...] - inner_rate * steps) * (1.0 / REPLICAS)
    new_momentum = nesterov_mu * momv[...] + mean_delta
    momn[...] = new_momentum
    ancn[...] = ancv[...] - outer_rate * (nesterov_mu * new_momentum + mean_delta)
    finish(1)

    cp_xl.wait_send()
    arrived(ysend.at[0:7, 0, 0], yl_ss)
    arrived(zsend, z_ss)
    arrived(sib, sib_ss)
    arrived(psend, p_ss)


def write_out(*refs):
    copies = [pltpu.make_async_copy(refs[i], refs[5 + i], refs[10].at[i]) for i in range(5)]
    for cp in copies:
        cp.start()
    for cp in copies:
        cp.wait()


def per_device(
    hidden_in, norm_gain, replica_weight, cotangent, adam_first, adam_second, anchor, outer_momentum
):
    any_space = pl.BlockSpec(memory_space=pl.ANY)
    dma = pltpu.SemaphoreType.DMA
    in_vmem = pl.BlockSpec(memory_space=pltpu.VMEM)
    rows = (NY, NZ, 32)
    results = [((2, 128, KV), BF), ((*rows, KV), F32), ((*rows, KV), F32), ((16, KV), F32), ((16, KV), F32)]
    outs = pl.pallas_call(
        kernel,
        name="diloco_step",
        out_shape=tuple(pltpu.VMEM(*o) for o in results),
        in_specs=[any_space] * 8,
        out_specs=[in_vmem] * 5,
        scratch_shapes=[
            pltpu.VMEM((256, 4096), BF),
            pltpu.VMEM((1, 4096), F32),
            pltpu.VMEM((*rows, KV), BF),
            pltpu.VMEM((2, 4, 128, KV), BF),
            pltpu.VMEM((*rows, KV), F32),
            pltpu.VMEM((*rows, KV), F32),
            pltpu.VMEM((16, KV), F32),
            pltpu.VMEM((16, KV), F32),
            pltpu.VMEM((256, 128), F32),
            pltpu.VMEM((3, 2, *rows, 128), BF),
            pltpu.VMEM((2, 4, *rows, 128), BF),
            pltpu.VMEM((4, 32, KV), F32),
            pltpu.VMEM((2, 4, KV, 128), F32),
            pltpu.VMEM((2, 2, KV, 128), F32),
            pltpu.VMEM((2, KV, 128), BF),
            pltpu.VMEM((2, KV, 128), BF),
            pltpu.VMEM((8, NY, 2, 16, KV), BF),
            pltpu.VMEM((7, NY, 2, 16, KV), BF),
            pltpu.VMEM((NY, 2, 16, KV), BF),
            pltpu.VMEM((NY, NZ, 32, KV), BF),
            pltpu.VMEM((7, 2, 16, KV), F32),
            pltpu.VMEM((7, 2, 16, KV), F32),
            pltpu.VMEM((2, 16, KV), F32),
            pltpu.VMEM((16, KV), F32),
            dma((8,)),
            dma((3,)), dma((3,)),
            dma, dma((9,)),
            dma, dma,
            dma, dma((7,)),
            dma, dma,
            dma, dma,
            dma, dma,
            dma, dma((2, 2, PIECES)),
            dma, dma((2, PIECES)),
        ],
        compiler_params=pltpu.CompilerParams(
            collective_id=0, has_side_effects=True, vmem_limit_bytes=52 << 20
        ),
        cost_estimate=pl.CostEstimate(
            flops=4 * 256 * 4096 * 512, bytes_accessed=12 << 20, transcendentals=1 << 20
        ),
    )(
        hidden_in.reshape(256, 4096),
        norm_gain.reshape(1, 4096),
        replica_weight.reshape(*rows, KV),
        cotangent.reshape(2, 128, KV),
        adam_first.reshape(*rows, KV),
        adam_second.reshape(*rows, KV),
        anchor,
        outer_momentum,
    )
    projected, first, second, new_anchor, new_momentum = pl.pallas_call(
        write_out,
        name="write_out",
        out_shape=tuple(jax.ShapeDtypeStruct(*o) for o in results),
        in_specs=[in_vmem] * 5,
        out_specs=[any_space] * 5,
        scratch_shapes=[dma((5,))],
        compiler_params=pltpu.CompilerParams(vmem_limit_bytes=1 << 20),
        cost_estimate=pl.CostEstimate(flops=0, bytes_accessed=5 << 20, transcendentals=0),
    )(*(pltpu.with_memory_space_constraint(o, pltpu.VMEM) for o in outs))
    return (
        projected.reshape(1, 256, KV),
        first.reshape(1, 1024, KV),
        second.reshape(1, 1024, KV),
        new_anchor,
        new_momentum,
    )


def solution(mesh):
    placed = (
        P("rep", "fsdp", None),
        P(),
        P("rep", "fsdp", None),
        P("rep", "fsdp", None),
        P("rep", "fsdp", None),
        P("rep", "fsdp", None),
        P(("fsdp", "rep"), None),
        P(("fsdp", "rep"), None),
    )
    return jax.shard_map(
        per_device,
        mesh=mesh,
        in_specs=placed,
        out_specs=(
            P("rep", "fsdp", None),
            P("rep", "fsdp", None),
            P("rep", "fsdp", None),
            P(("fsdp", "rep"), None),
            P(("fsdp", "rep"), None),
        ),
        check_vma=False,
    )
```
